32 devices in a mesh: rows: 4 (over y, x), cols: 8 (over z, core).
Axes of the slice: x: 2, y: 2, z: 4, core: 2. Of those that a mesh axis runs over, the one named last changes fastest.
Arguments:
- velocity: float32 [4, 512, 16384], P(None, 'rows', 'cols'), may hold values from -6 to 6
- layer_gap: float32 [512, 16384], P('rows', 'cols'), may hold values from -6 to 6
- surface: float32 [512, 16384], P('rows', 'cols'), may hold values from -3 to 3
- basin_depth: float32 [512, 16384], P('rows', 'cols'), may hold values from 0.25 to 1
- ocean_mask: int32 [512, 16384], P('rows', 'cols'), may hold values 0 or 1
Outputs:
- predicted: float32 [4, 512, 16384], P(None, 'rows', 'cols')
- new_surface: float32 [512, 16384], P('rows', 'cols')
The draws below stay inside these ranges and needn't reach their ends.
All inputs are finite; a program needn't handle non-finite values. No bound on the sum of `ocean_mask` on one device may be relied on, other than what follows from the above.
Results may differ from the reference program's by a relative error of at most 0.0003.
Values sent between devices are 32-bit elements; how exact they have to be, the bound alone decides.
A program may use at most 128 MiB of HBM per device.

```python
import math
import jax
import jax.numpy as jnp

NX = 16384
ITERS = 3
NY = 512
REACH = 4096


def draw_surface(key, part):
    key = jax.random.fold_in(key, 7)
    return jnp.clip(jax.random.normal(key, (NY, NX), jnp.float32), -3.0, 3.0)


def touch_ends(array, key, smallest, high):
    index_at = [jax.random.randint(jax.random.fold_in(key, axis), (), 0, length) for axis, length in enumerate(array.shape)]
    widest = array.shape.index(max(array.shape))
    beside = index_at[:widest] + [(index_at[widest] + 1) % array.shape[widest]] + index_at[widest + 1:]
    return array.at[tuple(index_at)].set(smallest).at[tuple(beside)].set(high)


def steps_of(rng, dims, split, least, largest):
    factor_of, own = 1.0, jax.random.fold_in(rng, 6)
    for position, parts in split:
        heights = jnp.exp(jax.random.uniform(jax.random.fold_in(own, position), (parts,), jnp.float32, least / len(split), largest / len(split)))
        factor_of = factor_of * jnp.repeat(heights, dims[position] // parts).reshape([-1 if axis == position else 1 for axis in range(len(dims))])
    return factor_of


def normal_values(own_key, dims, width, bound, pieces=(), kind=jnp.bfloat16):
    level = steps_of(own_key, dims, pieces, -0.22, 0.18) if pieces else 1.0
    values = jax.random.normal(own_key, dims, jnp.float32) * width * level
    return jnp.minimum(jnp.maximum(values, -bound), bound).astype(kind)


def setup_inputs(seed: int = 0) -> dict:
    key_of = jax.random.split(jax.random.key(seed), 6)
    velocity = normal_values(key_of[0], (4, NY, NX), 1.0, 6.0, ((1, 4), (2, 8)), jnp.float32)
    layer_gap = normal_values(key_of[1], (NY, NX), 1.0, 6.0, ((0, 4), (1, 8)), jnp.float32)
    surface = draw_surface(jax.random.fold_in(key_of[5], 71), 0)
    basin_depth = jnp.clip(jnp.exp(math.log(1.0) - 1.3862944 * jax.random.uniform(key_of[3], (NY, NX), jnp.float32) ** steps_of(key_of[3], (NY, NX), ((0, 4), (1, 8)), -0.2, 0.2)), 0.25, 1.0)
    ocean_mask = touch_ends((jax.random.randint(key_of[4], (NY, NX), 0, 5) < 4).astype(jnp.int32), jax.random.fold_in(key_of[4], 1), 0, 1)
    return {"velocity": velocity, "layer_gap": layer_gap, "surface": surface, "basin_depth": basin_depth, "ocean_mask": ocean_mask}


coriolis_dt = 0.1
viscous_dt = 0.05
buoyant_dt = 0.2
top_share = 0.3
transport_dt = 0.5
cross_weight = 0.5

def neighbour(padded, rim_width, margin, row_step, column_step):
    height = padded.shape[-2] - 2 * rim_width + 2 * margin
    breadth = padded.shape[-1] - 2 * rim_width + 2 * margin
    top_row = rim_width - margin + row_step
    left_column = rim_width - margin + column_step
    return padded[..., top_row:top_row + height, left_column:left_column + breadth]

def predict(padded, rim_width, margin):
    velocity = padded[:4]
    centre = neighbour(velocity, rim_width, margin, 0, 0)
    spread = neighbour(velocity, rim_width, margin, 0, 1) + neighbour(velocity, rim_width, margin, 0, -1) + neighbour(velocity, rim_width, margin, 1, 0) + neighbour(velocity, rim_width, margin, -1, 0) - 4.0 * centre
    layer_gap = padded[4]
    slope_east = 0.5 * (neighbour(layer_gap, rim_width, margin, 0, 1) - neighbour(layer_gap, rim_width, margin, 0, -1))
    slope_north = 0.5 * (neighbour(layer_gap, rim_width, margin, 1, 0) - neighbour(layer_gap, rim_width, margin, -1, 0))
    upper_east = centre[0] + coriolis_dt * centre[1] + viscous_dt * spread[0]
    upper_north = centre[1] - coriolis_dt * centre[0] + viscous_dt * spread[1]
    lower_east = centre[2] + coriolis_dt * centre[3] - buoyant_dt * slope_east + viscous_dt * spread[2]
    lower_north = centre[3] - coriolis_dt * centre[2] - buoyant_dt * slope_north + viscous_dt * spread[3]
    return jnp.stack([upper_east, upper_north, lower_east, lower_north])

def transports(predicted, column_depth):
    flux_east = column_depth * (top_share * predicted[0] + (1.0 - top_share) * predicted[2])
    flux_north = column_depth * (top_share * predicted[1] + (1.0 - top_share) * predicted[3])
    return jnp.stack([flux_east, flux_north])

def divergence(padded_flux):
    return 0.5 * (neighbour(padded_flux[0], 1, 0, 0, 1) - neighbour(padded_flux[0], 1, 0, 0, -1)) + 0.5 * (neighbour(padded_flux[1], 1, 0, 1, 0) - neighbour(padded_flux[1], 1, 0, -1, 0))

def operate(padded_surface, padded_depth, stiffness):
    centre = neighbour(padded_surface, 1, 0, 0, 0)
    depth_here = neighbour(padded_depth, 1, 0, 0, 0)
    result = centre
    for row_step, column_step, weight in ((0, 1, stiffness), (0, -1, stiffness), (1, 0, cross_weight), (-1, 0, cross_weight)):
        conductance = jnp.sqrt(depth_here * neighbour(padded_depth, 1, 0, row_step, column_step))
        result = result + weight * conductance * (centre - neighbour(padded_surface, 1, 0, row_step, column_step))
    return result

def line_solve(residual, stiffness):
    length = residual.shape[-1]
    mirrored = jnp.concatenate([residual, residual[:, ::-1]], axis=1)
    frequency = jnp.arange(length + 1).astype(residual.dtype)
    eigenvalue = 1.0 + 2.0 * cross_weight + 4.0 * stiffness * jnp.sin(jnp.pi * frequency / (2 * length)) ** 2
    spectrum = jnp.fft.rfft(mirrored, axis=1) / eigenvalue
    return jnp.fft.irfft(spectrum, n=2 * length, axis=1)[:, :length].astype(residual.dtype)

def reference(velocity, layer_gap, surface, basin_depth, ocean_mask):
    wet_cells = ocean_mask.astype(jnp.float32)
    wet_depth = basin_depth * wet_cells
    stiffness = (1.0 + 2.0 * cross_weight) * REACH ** 2
    state_stack = jnp.concatenate([velocity, layer_gap[None], wet_depth[None]], axis=0)
    padded = jnp.pad(state_stack, ((0, 0), (1, 1), (1, 1)))
    predicted = predict(padded, 1, 0) * wet_cells
    padded_flux = jnp.pad(transports(predicted, wet_depth), ((0, 0), (1, 1), (1, 1)))
    forcing = wet_cells * (surface - transport_dt * divergence(padded_flux))
    padded_depth = padded[5]
    surface_level = jnp.zeros_like(surface)
    residual = forcing
    for iteration in range(ITERS):
        surface_level = surface_level + wet_cells * line_solve(residual, stiffness)
        if iteration + 1 < ITERS:
            residual = wet_cells * (forcing - operate(jnp.pad(surface_level, 1), padded_depth, stiffness))
    return (predicted, math.sqrt(REACH) * surface_level)
```

```python
import functools
import math

import jax
import jax.numpy as jnp
import numpy as np
from jax import lax
from jax.experimental import pallas as pl
from jax.experimental.pallas import tpu as pltpu
from jax.sharding import PartitionSpec as P

ITERS = 3
REACH = 4096
BLOCK = 128
PAD = 8

coriolis_dt = 0.1
viscous_dt = 0.05
buoyant_dt = 0.2
top_share = 0.3
transport_dt = 0.5
cross_weight = 0.5
F32 = jnp.float32
MESH = pl.DeviceIdType.MESH
EXACT = lax.Precision.HIGHEST


def line_constants():
    base = 1.0 + 2.0 * cross_weight
    stiffness = base * REACH**2
    root = math.sqrt(base * base + 4.0 * base * stiffness)
    lag = (base + root) / (base + 2.0 * stiffness + root)
    gain = 1.0 / (base + 2.0 * stiffness * lag)
    return stiffness, lag, gain


def tables(length, count):
    _, lag, _ = line_constants()
    log = math.log1p(-lag)
    power = lambda n: np.exp(np.asarray(n, np.float64) * log)
    lane = np.arange(BLOCK)
    gap = lane[None, :] - lane[:, None]
    onward = np.where(gap >= 0, power(np.maximum(gap, 0)), 0.0)
    within = np.concatenate([onward, onward.T], axis=1)
    cell = np.arange(length)
    blocks = length // BLOCK
    gather = np.zeros((length, BLOCK))
    gather[:, 0] = gather[:, 3] = power(length - 1 - cell)
    gather[:, 1] = gather[:, 2] = power(cell)
    spread = np.zeros((BLOCK, BLOCK))
    for b in range(blocks):
        west, east = b * BLOCK, (b + 1) * BLOCK
        gather[:west, 8 + b] = power(west - 1 - cell[:west])
        gather[east:, 40 + b] = power(cell[east:] - east)
        spread[0, 8 + b] = spread[2, 8 + b] = power(west)
        spread[1, 40 + b] = spread[3, 40 + b] = power(length - east)
    q = float(power(length * count))
    hop = np.zeros((count, 8, BLOCK))
    for me in range(count):
        for k in range(count):
            p = (me - k) % count
            first, last = float(power(p * length)), float(power((count - 1 - p) * length))
            west_in, east_in = float(power(me * length)), float(power((count - 1 - me) * length))
            hop[me, 0, k] = west_in * q * last / (1 - q * q)
            hop[me, 2, k] = west_in * first / (1 - q * q)
            hop[me, 1, k] = east_in * q * first / (1 - q * q)
            hop[me, 3, k] = east_in * last / (1 - q * q)
            if p < me:
                hop[me, 0, k] += float(power((me - 1 - p) * length))
            if p > me:
                hop[me, 1, k] += float(power((p - me - 1) * length))
    edge = np.zeros((8, BLOCK))
    edge[0] = power(lane + 1)
    edge[1] = power(BLOCK - lane)
    return [np.asarray(a, np.float32) for a in (gather, within, spread, hop, edge)]


def transposed(rows8):
    return jnp.concatenate([rows8, jnp.zeros((BLOCK - 8, BLOCK), F32)], axis=0).T


def kernel(
    row_count, col_count, height, length,
    vel_hbm, gap_hbm, surf_hbm, depth_hbm, mask_hbm, gather_hbm,
    within, spread, hop, edge,
    pred_hbm, out_hbm,
    vel, gap, wd, mask, surf, gather, pred, fe, fn, ce, cw, cn, cs, res, on, bk, dl, lev, car,
    row_send, row_recv, col_send, col_recv, colw, cole, frow_send, frow_recv, fcol_send, fcol_recv,
    sum_send, sum_recv, drow_send, drow_recv,
    load_sem, out_sem, halo_ss, halo_rs, fh_ss, fh_rs, sum_ss, sum_rs, d_ss, d_rs,
):
    row = lax.axis_index("rows")
    col = lax.axis_index("cols")
    tiles = height // 8
    blocks = length // BLOCK
    stiffness, lag, gain = line_constants()
    decay = 1.0 - lag
    own = pl.ds(PAD, height)

    loads = [
        pltpu.make_async_copy(depth_hbm, wd.at[own], load_sem.at[0]),
        pltpu.make_async_copy(mask_hbm, mask, load_sem.at[1]),
        pltpu.make_async_copy(gap_hbm, gap.at[own], load_sem.at[2]),
        pltpu.make_async_copy(vel_hbm, vel.at[:, own], load_sem.at[3]),
        pltpu.make_async_copy(surf_hbm, surf, load_sem.at[4]),
        pltpu.make_async_copy(gather_hbm, gather, load_sem.at[5]),
    ]
    for load in loads:
        load.start()

    has_n, has_s = row > 0, row < row_count - 1
    has_w, has_e = col > 0, col < col_count - 1
    peers = [lax.rem(col + k, col_count) for k in range(1, col_count)]
    barrier = pltpu.get_barrier_semaphore()
    for peer in peers:
        pl.semaphore_signal(barrier, inc=1, device_id={"cols": peer}, device_id_type=MESH)

    @pl.when(has_n)
    def _():
        pl.semaphore_signal(barrier, inc=1, device_id={"rows": row - 1}, device_id_type=MESH)

    @pl.when(has_s)
    def _():
        pl.semaphore_signal(barrier, inc=1, device_id={"rows": row + 1}, device_id_type=MESH)

    neighbours = jnp.minimum(row, 1) + jnp.minimum(row_count - 1 - row, 1)
    pl.semaphore_wait(barrier, col_count - 1 + neighbours)

    def copies(send, recv, send_sem, recv_sem, axis, place):
        return [
            pltpu.make_async_remote_copy(
                src_ref=send.at[side], dst_ref=recv.at[1 - side],
                send_sem=send_sem.at[side], recv_sem=recv_sem.at[1 - side],
                device_id={axis: place + (2 * side - 1)}, device_id_type=MESH,
            )
            for side in range(2)
        ]

    def start(pair, low, high):
        pl.when(low)(pair[0].start)
        pl.when(high)(pair[1].start)

    def finish(pair, recv, low, high):
        for side, there in ((0, low), (1, high)):
            @pl.when(there)
            def _():
                pair[1 - side].wait_recv()
                pair[side].wait_send()

            @pl.when(jnp.logical_not(there))
            def _():
                recv[side] = jnp.zeros(recv.shape[1:], F32)

    row_halo = copies(row_send, row_recv, halo_ss.at[0], halo_rs.at[0], "rows", row)
    col_halo = copies(col_send, col_recv, halo_ss.at[1], halo_rs.at[1], "cols", col)
    frow_halo = copies(frow_send, frow_recv, fh_ss.at[0], fh_rs.at[0], "rows", row)
    fcol_halo = copies(fcol_send, fcol_recv, fh_ss.at[1], fh_rs.at[1], "cols", col)

    loads[0].wait()
    loads[1].wait()

    def wetten(t, carry):
        at = pl.ds(pl.multiple_of(PAD + 8 * t, 8), 8)
        wd[at, :] = wd[at, :] * mask[pl.ds(pl.multiple_of(8 * t, 8), 8), :].astype(F32)
        return carry

    lax.fori_loop(0, tiles, wetten, 0)
    loads[2].wait()
    loads[3].wait()

    fields = [vel.at[0], vel.at[1], vel.at[2], vel.at[3], gap, wd]
    lane = lax.broadcasted_iota(jnp.int32, (height, BLOCK), 1)
    west_pack = jnp.zeros((height, BLOCK), F32)
    east_pack = jnp.zeros((height, BLOCK), F32)
    for k, field in enumerate(fields):
        row_send[0, k : k + 1, :] = field[PAD : PAD + 1, :]
        row_send[1, k : k + 1, :] = field[PAD + height - 1 : PAD + height, :]
    start(row_halo, has_n, has_s)
    for k, field in enumerate(fields):
        low = field[PAD : PAD + height, 0:BLOCK]
        high = field[PAD : PAD + height, length - BLOCK : length]
        west_pack = jnp.where(lane == k, low if k == 0 else pltpu.roll(low, k, 1), west_pack)
        east_pack = jnp.where(lane == k, pltpu.roll(high, k + 1, 1), east_pack)
    col_send[0] = west_pack.T[0:8]
    col_send[1] = east_pack.T[0:8]
    start(col_halo, has_w, has_e)
    finish(row_halo, row_recv, has_n, has_s)
    finish(col_halo, col_recv, has_w, has_e)
    for k, field in enumerate(fields):
        field[PAD - 1 : PAD, :] = row_recv[0, k : k + 1, :]
        field[PAD + height : PAD + height + 1, :] = row_recv[1, k : k + 1, :]
    colw[...] = transposed(col_recv[0])
    cole[...] = transposed(col_recv[1])

    wide = lax.broadcasted_iota(jnp.int32, (8, length), 1)
    at_west, at_east = wide == 0, wide == length - 1

    def west_of(x, edge_column):
        return jnp.where(at_west, edge_column, pltpu.roll(x, 1, 1))

    def east_of(x, edge_column):
        return jnp.where(at_east, edge_column, pltpu.roll(x, length - 1, 1))

    def rows_of(t):
        return pl.ds(pl.multiple_of(8 * t, 8), 8)

    sub = lax.broadcasted_iota(jnp.int32, (8, length), 0)

    def three(ref, t):
        before = ref[rows_of(t), :]
        here = ref[rows_of(t + 1), :]
        after = ref[rows_of(t + 2), :]
        north = jnp.where(sub == 0, pltpu.roll(before, 1, 0), pltpu.roll(here, 1, 0))
        south = jnp.where(sub == 7, pltpu.roll(after, 7, 0), pltpu.roll(here, 7, 0))
        return here, north, south

    def momentum(t, carry):
        at = rows_of(t)
        depth_here = wd[rows_of(t + 1), :]
        wet = jnp.where(depth_here > 0.0, 1.0, 0.0)
        west_halo, east_halo = colw[at, :], cole[at, :]
        gap_here, gap_north, gap_south = three(gap, t)
        slope_east = 0.5 * (
            east_of(gap_here, east_halo[:, 4:5]) - west_of(gap_here, west_halo[:, 4:5])
        )
        slope_north = 0.5 * (gap_south - gap_north)
        for pair in range(2):
            parts = []
            for side in range(2):
                k = 2 * pair + side
                here, north, south = three(vel.at[k], t)
                lap = (
                    east_of(here, east_halo[:, k : k + 1])
                    + west_of(here, west_halo[:, k : k + 1])
                    + south + north - 4.0 * here
                )
                parts.append(here + viscous_dt * lap)
            u, v = vel[2 * pair, rows_of(t + 1), :], vel[2 * pair + 1, rows_of(t + 1), :]
            east = parts[0] + coriolis_dt * v
            north_part = parts[1] - coriolis_dt * u
            if pair == 1:
                east = east - buoyant_dt * slope_east
                north_part = north_part - buoyant_dt * slope_north
            pred[2 * pair, at, :] = wet * east
            pred[2 * pair + 1, at, :] = wet * north_part
        fe[at, :] = depth_here * (top_share * pred[0, at, :] + (1.0 - top_share) * pred[2, at, :])
        fn[rows_of(t + 1), :] = depth_here * (
            top_share * pred[1, at, :] + (1.0 - top_share) * pred[3, at, :]
        )
        return carry

    lax.fori_loop(0, tiles, momentum, 0)
    pred_out = pltpu.make_async_copy(pred, pred_hbm, out_sem.at[0])
    pred_out.start()

    frow_send[0] = fn[PAD : PAD + 1, :]
    frow_send[1] = fn[PAD + height - 1 : PAD + height, :]
    start(frow_halo, has_n, has_s)
    fcol_send[0] = fe[:, 0:BLOCK].T[0:8]
    fcol_send[1] = pltpu.roll(fe[:, length - BLOCK : length], 1, 1).T[0:8]
    start(fcol_halo, has_w, has_e)

    def conductances(t, carry):
        at = rows_of(t)
        here, north, south = three(wd, t)
        ce[at, :] = jnp.sqrt(here * east_of(here, cole[at, 5:6]))
        cw[at, :] = jnp.sqrt(here * west_of(here, colw[at, 5:6]))
        cn[at, :] = cross_weight * jnp.sqrt(here * north)
        cs[at, :] = cross_weight * jnp.sqrt(here * south)
        return carry

    lax.fori_loop(0, tiles, conductances, 0)
    finish(frow_halo, frow_recv, has_n, has_s)
    finish(fcol_halo, fcol_recv, has_w, has_e)
    fn[PAD - 1 : PAD, :] = frow_recv[0]
    fn[PAD + height : PAD + height + 1, :] = frow_recv[1]
    colw[...] = transposed(fcol_recv[0])
    cole[...] = transposed(fcol_recv[1])
    loads[4].wait()
    loads[5].wait()

    def force(t, carry):
        at = rows_of(t)
        east_flux = fe[at, :]
        _, north, south = three(fn, t)
        divergence = 0.5 * (
            east_of(east_flux, cole[at, 0:1]) - west_of(east_flux, colw[at, 0:1])
        ) + 0.5 * (south - north)
        wet = wd[rows_of(t + 1), :] > 0.0
        res[at, :] = jnp.where(wet, surf[at, :] - transport_dt * divergence, 0.0)
        return carry

    lax.fori_loop(0, tiles, force, 0)

    hop_here = hop[col]
    for it in range(ITERS):
        last = it + 1 == ITERS
        sums = jnp.dot(res[...], gather[...], precision=EXACT, preferred_element_type=F32)
        sum_send[it] = sums.T[0:8]
        sends = [
            pltpu.make_async_remote_copy(
                src_ref=sum_send.at[it], dst_ref=sum_recv.at[it, k],
                send_sem=sum_ss.at[it, k], recv_sem=sum_rs.at[it, k],
                device_id={"cols": peers[k - 1]}, device_id_type=MESH,
            )
            for k in range(1, col_count)
        ]
        for send in sends:
            send.start()

        for b in range(blocks):
            at = slice(b * BLOCK, (b + 1) * BLOCK)
            both = jnp.dot(res[:, at], within[...], precision=EXACT, preferred_element_type=F32)
            on[:, at] = both[:, :BLOCK]
            bk[:, at] = both[:, BLOCK:]

        entering = hop_here[:, 0:1] * sum_send[it]
        for k in range(1, col_count):
            sends[k - 1].wait_recv()
            entering = entering + hop_here[:, k : k + 1] * sum_recv[it, k]
        car[...] = sums + jnp.dot(
            transposed(entering), spread[...], precision=EXACT, preferred_element_type=F32
        )

        rising = jnp.broadcast_to(edge[0:1, :], (8, BLOCK))
        falling = jnp.broadcast_to(edge[1:2, :], (8, BLOCK))

        def solve(t, carry):
            at = rows_of(t)
            inner = rows_of(t + 1)
            enter = car[at, :]
            for b in range(blocks):
                cells = slice(b * BLOCK, (b + 1) * BLOCK)
                r = res[at, cells]
                o = on[at, cells] + rising * enter[:, 8 + b : 9 + b]
                w = bk[at, cells] + falling * enter[:, 40 + b : 41 + b]
                wet = wd[inner, cells] > 0.0
                d = jnp.where(wet, gain * (o + w - r), 0.0)
                if last:
                    lev[at, cells] = math.sqrt(REACH) * (lev[at, cells] + d)
                    continue
                if it == 0:
                    lev[at, cells] = d
                else:
                    lev[at, cells] = lev[at, cells] + d
                dl[inner, cells] = d
                flux_e = (w - r) * (1.0 / decay) - o
                flux_w = w - (o - r) * (1.0 / decay)
                scale = stiffness * gain * lag
                res[at, cells] = (
                    r - d + scale * (ce[at, cells] * flux_e - cw[at, cells] * flux_w)
                )
            return carry

        if last:
            lax.fori_loop(0, tiles, solve, 0)
            for send in sends:
                send.wait_send()
            break

        solve(0, 0)
        solve(tiles - 1, 0)
        drow_send[it, 0] = dl[PAD : PAD + 1, :]
        drow_send[it, 1] = dl[PAD + height - 1 : PAD + height, :]
        d_halo = copies(
            drow_send.at[it], drow_recv.at[it], d_ss.at[it], d_rs.at[it], "rows", row
        )
        start(d_halo, has_n, has_s)
        lax.fori_loop(1, tiles - 1, solve, 0)

        def cross(t, carry):
            at = rows_of(t)
            here, north, south = three(dl, t)
            value = res[at, :] - cn[at, :] * (here - north) - cs[at, :] * (here - south)
            res[at, :] = jnp.where(wd[rows_of(t + 1), :] > 0.0, value, 0.0)
            return carry

        lax.fori_loop(1, tiles - 1, cross, 0)
        finish(d_halo, drow_recv.at[it], has_n, has_s)
        dl[PAD - 1 : PAD, :] = drow_recv[it, 0]
        dl[PAD + height : PAD + height + 1, :] = drow_recv[it, 1]
        cross(0, 0)
        cross(tiles - 1, 0)
        for send in sends:
            send.wait_send()

    out = pltpu.make_async_copy(lev, out_hbm, out_sem.at[1])
    out.start()
    out.wait()
    pred_out.wait()


def per_device(row_count, col_count, velocity, layer_gap, surface, basin_depth, ocean_mask):
    height, length = surface.shape
    gather, within, spread, hop, edge = tables(length, col_count)
    padded = pltpu.VMEM((height + 2 * PAD, length), F32)
    plain = pltpu.VMEM((height, length), F32)
    tile = pltpu.VMEM((height, BLOCK), F32)
    dma = pltpu.SemaphoreType.DMA
    anywhere = pl.BlockSpec(memory_space=pl.ANY)
    vmem = pl.BlockSpec(memory_space=pltpu.VMEM)
    predicted, level = pl.pallas_call(
        functools.partial(kernel, row_count, col_count, height, length),
        out_shape=(
            jax.ShapeDtypeStruct(velocity.shape, F32),
            jax.ShapeDtypeStruct(surface.shape, F32),
        ),
        in_specs=[anywhere] * 6 + [vmem] * 4,
        out_specs=(anywhere, anywhere),
        scratch_shapes=[
            pltpu.VMEM((4, height + 2 * PAD, length), F32),
            padded, padded, pltpu.VMEM((height, length), jnp.int32), plain,
            pltpu.VMEM((length, BLOCK), F32),
            pltpu.VMEM((4, height, length), F32),
            plain, padded, plain, plain, plain, plain, plain, plain, plain, padded, plain, tile,
            pltpu.VMEM((2, 8, length), F32), pltpu.VMEM((2, 8, length), F32),
            pltpu.VMEM((2, 8, BLOCK), F32), pltpu.VMEM((2, 8, BLOCK), F32),
            tile, tile,
            pltpu.VMEM((2, 1, length), F32), pltpu.VMEM((2, 1, length), F32),
            pltpu.VMEM((2, 8, BLOCK), F32), pltpu.VMEM((2, 8, BLOCK), F32),
            pltpu.VMEM((ITERS, 8, BLOCK), F32), pltpu.VMEM((ITERS, col_count, 8, BLOCK), F32),
            pltpu.VMEM((ITERS, 2, 1, length), F32), pltpu.VMEM((ITERS, 2, 1, length), F32),
            dma((6,)), dma((2,)), dma((2, 2)), dma((2, 2)), dma((2, 2)), dma((2, 2)),
            dma((ITERS, col_count)), dma((ITERS, col_count)), dma((ITERS, 2)), dma((ITERS, 2)),
        ],
        compiler_params=pltpu.CompilerParams(
            collective_id=0, has_side_effects=True, vmem_limit_bytes=50 * 2**20
        ),
    )(velocity, layer_gap, surface, basin_depth, ocean_mask, gather, within, spread, hop, edge)
    return predicted, level


def solution(mesh):
    placed = (P(None, "rows", "cols"),) + (P("rows", "cols"),) * 4
    return jax.shard_map(
        functools.partial(per_device, mesh.shape["rows"], mesh.shape["cols"]),
        mesh=mesh,
        in_specs=placed,
        out_specs=(P(None, "rows", "cols"), P("rows", "cols")),
        check_vma=False,
    )
```

```python
import functools
import math

import jax
import jax.numpy as jnp
import numpy as np
from jax import lax
from jax.experimental import pallas as pl
from jax.experimental.pallas import tpu as pltpu
from jax.sharding import PartitionSpec as P

ITERS = 3
REACH = 4096
BLOCK = 128
PAD = 8

coriolis_dt = 0.1
viscous_dt = 0.05
buoyant_dt = 0.2
top_share = 0.3
transport_dt = 0.5
cross_weight = 0.5
F32 = jnp.float32
MESH = pl.DeviceIdType.MESH
EXACT = lax.Precision.HIGHEST


def line_constants():
    base = 1.0 + 2.0 * cross_weight
    stiffness = base * REACH**2
    root = math.sqrt(base * base + 4.0 * base * stiffness)
    lag = (base + root) / (base + 2.0 * stiffness + root)
    gain = 1.0 / (base + 2.0 * stiffness * lag)
    return stiffness, lag, gain


def tables(length, count):
    _, lag, _ = line_constants()
    log = math.log1p(-lag)
    power = lambda n: np.exp(np.asarray(n, np.float64) * log)
    lane = np.arange(BLOCK)
    gap = lane[None, :] - lane[:, None]
    onward = np.where(gap >= 0, power(np.maximum(gap, 0)), 0.0)
    within = np.concatenate([onward, onward.T], axis=1)
    cell = np.arange(length)
    blocks = length // BLOCK
    gather = np.zeros((length, BLOCK))
    gather[:, 0] = gather[:, 3] = power(length - 1 - cell)
    gather[:, 1] = gather[:, 2] = power(cell)
    spread = np.zeros((BLOCK, BLOCK))
    for b in range(blocks):
        west, east = b * BLOCK, (b + 1) * BLOCK
        gather[:west, 8 + b] = power(west - 1 - cell[:west])
        gather[east:, 40 + b] = power(cell[east:] - east)
        spread[0, 8 + b] = spread[2, 8 + b] = power(west)
        spread[1, 40 + b] = spread[3, 40 + b] = power(length - east)
    q = float(power(length * count))
    hop = np.zeros((count, 8, BLOCK))
    for me in range(count):
        for k in range(count):
            p = (me - k) % count
            first, last = float(power(p * length)), float(power((count - 1 - p) * length))
            west_in, east_in = float(power(me * length)), float(power((count - 1 - me) * length))
            hop[me, 0, k] = west_in * q * last / (1 - q * q)
            hop[me, 2, k] = west_in * first / (1 - q * q)
            hop[me, 1, k] = east_in * q * first / (1 - q * q)
            hop[me, 3, k] = east_in * last / (1 - q * q)
            if p < me:
                hop[me, 0, k] += float(power((me - 1 - p) * length))
            if p > me:
                hop[me, 1, k] += float(power((p - me - 1) * length))
    edge = np.zeros((8, BLOCK))
    edge[0] = power(lane + 1)
    edge[1] = power(BLOCK - lane)
    def split(a):
        high = np.asarray(a, np.float32).astype(jnp.bfloat16)
        return high, (a - high.astype(np.float64)).astype(np.float32).astype(jnp.bfloat16)

    within_high, within_low = split(within)
    halves = np.concatenate(
        [np.concatenate(split(gather), axis=1), within_high, within_high, within_low],
        axis=0,
    )
    exact = np.concatenate([spread, edge, hop.reshape(count * 8, BLOCK)]).astype(np.float32)
    return halves.astype(np.float32), exact


def transposed(rows8):
    return jnp.concatenate([rows8, jnp.zeros((BLOCK - 8, BLOCK), F32)], axis=0).T


def kernel(
    row_count, col_count, height, length,
    vel_hbm, gap_hbm, surf_hbm, depth_hbm, mask_hbm, halves_hbm, exact_hbm,
    pred_hbm, out_hbm,
    vel, gap, wd, mask, surf, wide_halves, halves, exact, vel_col, gap_col, depth_col, mask_col, split, pred, fe, fn, ce, cw, cn, cs, res, on, bk, dl, lev, car,
    row_send, row_recv, col_send, col_recv, colw, cole, frow_send, frow_recv, fcol_send, fcol_recv,
    sum_send, sum_recv, drow_send, drow_recv,
    load_sem, out_sem, halo_ss, halo_rs, fh_ss, fh_rs, sum_ss, sum_rs, d_ss, d_rs,
):
    row = lax.axis_index("rows")
    col = lax.axis_index("cols")
    tiles = height // 8
    blocks = length // BLOCK
    stiffness, lag, gain = line_constants()
    decay = 1.0 - lag

    middle = height - 16
    sources = (
        (depth_hbm, wd, depth_col, PAD, ()),
        (mask_hbm, mask, mask_col, 0, ()),
        (gap_hbm, gap, gap_col, PAD, ()),
        (vel_hbm, vel, vel_col, PAD, (slice(None),)),
    )
    pairs = []
    for start_row, size in ((0, 8), (height - 8, 8)):
        for hbm, held, _, pad, lead in sources:
            pairs.append((
                hbm.at[lead + (pl.ds(start_row, size),)],
                held.at[lead + (pl.ds(pad + start_row, size),)],
            ))
    for side, first in enumerate((0, length - BLOCK)):
        for hbm, _, held, pad, lead in sources:
            pairs.append((
                hbm.at[lead + (slice(None), pl.ds(first, BLOCK))], held.at[side]
            ))
    for hbm, held, _, pad, lead in sources:
        pairs.append((
            hbm.at[lead + (pl.ds(8, middle),)], held.at[lead + (pl.ds(pad + 8, middle),)]
        ))
    pairs += [(surf_hbm, surf), (halves_hbm, wide_halves), (exact_hbm, exact)]
    loads = [
        pltpu.make_async_copy(src, dst, load_sem.at[i]) for i, (src, dst) in enumerate(pairs)
    ]
    for load in loads:
        load.start()

    has_n, has_s = row > 0, row < row_count - 1
    has_w, has_e = col > 0, col < col_count - 1
    peers = [lax.rem(col + k, col_count) for k in range(1, col_count)]
    barrier = pltpu.get_barrier_semaphore()
    for peer in peers:
        pl.semaphore_signal(barrier, inc=1, device_id={"cols": peer}, device_id_type=MESH)

    @pl.when(has_n)
    def _():
        pl.semaphore_signal(barrier, inc=1, device_id={"rows": row - 1}, device_id_type=MESH)

    @pl.when(has_s)
    def _():
        pl.semaphore_signal(barrier, inc=1, device_id={"rows": row + 1}, device_id_type=MESH)

    neighbours = jnp.minimum(row, 1) + jnp.minimum(row_count - 1 - row, 1)
    pl.semaphore_wait(barrier, col_count - 1 + neighbours)

    def copies(send, recv, send_sem, recv_sem, axis, place):
        return [
            pltpu.make_async_remote_copy(
                src_ref=send.at[side], dst_ref=recv.at[1 - side],
                send_sem=send_sem.at[side], recv_sem=recv_sem.at[1 - side],
                device_id={axis: place + (2 * side - 1)}, device_id_type=MESH,
            )
            for side in range(2)
        ]

    def start(pair, low, high):
        pl.when(low)(pair[0].start)
        pl.when(high)(pair[1].start)

    def finish(pair, recv, low, high):
        for side, there in ((0, low), (1, high)):
            @pl.when(there)
            def _():
                pair[1 - side].wait_recv()
                pair[side].wait_send()

            @pl.when(jnp.logical_not(there))
            def _():
                recv[side] = jnp.zeros(recv.shape[1:], F32)

    row_halo = copies(row_send, row_recv, halo_ss.at[0], halo_rs.at[0], "rows", row)
    col_halo = copies(col_send, col_recv, halo_ss.at[1], halo_rs.at[1], "cols", col)
    frow_halo = copies(frow_send, frow_recv, fh_ss.at[0], fh_rs.at[0], "rows", row)
    fcol_halo = copies(fcol_send, fcol_recv, fh_ss.at[1], fh_rs.at[1], "cols", col)

    for load in loads[:8]:
        load.wait()
    for side, at in ((0, 0), (1, height - 1)):
        for k in range(4):
            row_send[side, k : k + 1, :] = vel[k, PAD + at : PAD + at + 1, :]
        row_send[side, 4:5, :] = gap[PAD + at : PAD + at + 1, :]
        row_send[side, 5:6, :] = (
            wd[PAD + at : PAD + at + 1, :] * mask[at : at + 1, :].astype(F32)
        )
    start(row_halo, has_n, has_s)
    for load in loads[8:16]:
        load.wait()
    lane = lax.broadcasted_iota(jnp.int32, (height, BLOCK), 1)
    for side in range(2):
        columns = [vel_col[side, k] for k in range(4)]
        columns += [gap_col[side], depth_col[side] * mask_col[side].astype(F32)]
        pack = jnp.zeros((height, BLOCK), F32)
        for k, column in enumerate(columns):
            pack = jnp.where(
                lane == k, column if k + side == 0 else pltpu.roll(column, k + side, 1), pack
            )
        col_send[side] = pack.T[0:8]
    start(col_halo, has_w, has_e)
    for load in loads[16:20]:
        load.wait()

    def wetten(t, carry):
        at = pl.ds(pl.multiple_of(PAD + 8 * t, 8), 8)
        wd[at, :] = wd[at, :] * mask[pl.ds(pl.multiple_of(8 * t, 8), 8), :].astype(F32)
        return carry

    lax.fori_loop(0, tiles, wetten, 0)
    fields = [vel.at[0], vel.at[1], vel.at[2], vel.at[3], gap, wd]
    finish(row_halo, row_recv, has_n, has_s)
    finish(col_halo, col_recv, has_w, has_e)
    for k, field in enumerate(fields):
        field[PAD - 1 : PAD, :] = row_recv[0, k : k + 1, :]
        field[PAD + height : PAD + height + 1, :] = row_recv[1, k : k + 1, :]
    colw[...] = transposed(col_recv[0])
    cole[...] = transposed(col_recv[1])

    wide = lax.broadcasted_iota(jnp.int32, (8, length), 1)
    at_west, at_east = wide == 0, wide == length - 1

    def west_of(x, edge_column):
        return jnp.where(at_west, edge_column, pltpu.roll(x, 1, 1))

    def east_of(x, edge_column):
        return jnp.where(at_east, edge_column, pltpu.roll(x, length - 1, 1))

    def rows_of(t):
        return pl.ds(pl.multiple_of(8 * t, 8), 8)

    sub = lax.broadcasted_iota(jnp.int32, (8, length), 0)

    def three(ref, t):
        before = ref[rows_of(t), :]
        here = ref[rows_of(t + 1), :]
        after = ref[rows_of(t + 2), :]
        north = pltpu.roll(jnp.where(sub == 7, before, here), 1, 0)
        south = pltpu.roll(jnp.where(sub == 0, after, here), 7, 0)
        return here, north, south

    def momentum(t, carry):
        at = rows_of(t)
        depth_here = wd[rows_of(t + 1), :]
        wet = jnp.where(depth_here > 0.0, 1.0, 0.0)
        west_halo, east_halo = colw[at, :], cole[at, :]
        gap_here, gap_north, gap_south = three(gap, t)
        slope_east = 0.5 * (
            east_of(gap_here, east_halo[:, 4:5]) - west_of(gap_here, west_halo[:, 4:5])
        )
        slope_north = 0.5 * (gap_south - gap_north)
        for pair in range(2):
            parts = []
            for side in range(2):
                k = 2 * pair + side
                here, north, south = three(vel.at[k], t)
                lap = (
                    east_of(here, east_halo[:, k : k + 1])
                    + west_of(here, west_halo[:, k : k + 1])
                    + south + north - 4.0 * here
                )
                parts.append(here + viscous_dt * lap)
            u, v = vel[2 * pair, rows_of(t + 1), :], vel[2 * pair + 1, rows_of(t + 1), :]
            east = parts[0] + coriolis_dt * v
            north_part = parts[1] - coriolis_dt * u
            if pair == 1:
                east = east - buoyant_dt * slope_east
                north_part = north_part - buoyant_dt * slope_north
            pred[2 * pair, at, :] = wet * east
            pred[2 * pair + 1, at, :] = wet * north_part
        fe[at, :] = depth_here * (top_share * pred[0, at, :] + (1.0 - top_share) * pred[2, at, :])
        fn[rows_of(t + 1), :] = depth_here * (
            top_share * pred[1, at, :] + (1.0 - top_share) * pred[3, at, :]
        )
        return carry

    lax.fori_loop(0, tiles, momentum, 0)
    pred_out = pltpu.make_async_copy(pred, pred_hbm, out_sem.at[0])
    pred_out.start()

    frow_send[0] = fn[PAD : PAD + 1, :]
    frow_send[1] = fn[PAD + height - 1 : PAD + height, :]
    start(frow_halo, has_n, has_s)
    fcol_send[0] = fe[:, 0:BLOCK].T[0:8]
    fcol_send[1] = pltpu.roll(fe[:, length - BLOCK : length], 1, 1).T[0:8]
    start(fcol_halo, has_w, has_e)

    def conductances(t, carry):
        at = rows_of(t)
        here, north, south = three(wd, t)
        ce[at, :] = jnp.sqrt(here * east_of(here, cole[at, 5:6]))
        cw[at, :] = jnp.sqrt(here * west_of(here, colw[at, 5:6]))
        cn[at, :] = cross_weight * jnp.sqrt(here * north)
        cs[at, :] = cross_weight * jnp.sqrt(here * south)
        return carry

    lax.fori_loop(0, tiles, conductances, 0)
    for load in loads[20:]:
        load.wait()

    def narrow(t, carry):
        at = pl.ds(pl.multiple_of(BLOCK * t, BLOCK), BLOCK)
        halves[at, :] = wide_halves[at, :].astype(jnp.bfloat16)
        return carry

    lax.fori_loop(0, blocks + 3, narrow, 0)
    finish(frow_halo, frow_recv, has_n, has_s)
    finish(fcol_halo, fcol_recv, has_w, has_e)
    fn[PAD - 1 : PAD, :] = frow_recv[0]
    fn[PAD + height : PAD + height + 1, :] = frow_recv[1]
    colw[...] = transposed(fcol_recv[0])
    cole[...] = transposed(fcol_recv[1])

    def force(t, carry):
        at = rows_of(t)
        east_flux = fe[at, :]
        _, north, south = three(fn, t)
        divergence = 0.5 * (
            east_of(east_flux, cole[at, 0:1]) - west_of(east_flux, colw[at, 0:1])
        ) + 0.5 * (south - north)
        wet = wd[rows_of(t + 1), :] > 0.0
        res[at, :] = jnp.where(wet, surf[at, :] - transport_dt * divergence, 0.0)
        return carry

    lax.fori_loop(0, tiles, force, 0)

    hop_here = exact[pl.ds(pl.multiple_of(BLOCK + 8 + 8 * col, 8), 8), :]
    rising = jnp.broadcast_to(exact[BLOCK : BLOCK + 1, :], (8, BLOCK))
    falling = jnp.broadcast_to(exact[BLOCK + 1 : BLOCK + 2, :], (8, BLOCK))
    dot = functools.partial(jnp.dot, preferred_element_type=F32)
    for it in range(ITERS):
        last = it + 1 == ITERS
        for b in range(blocks):
            at = slice(b * BLOCK, (b + 1) * BLOCK)
            high = res[:, at].astype(jnp.bfloat16)
            split[b, :, :BLOCK] = high
            split[b, :, BLOCK:] = (res[:, at] - high.astype(F32)).astype(jnp.bfloat16)
        total = jnp.zeros((height, 2 * BLOCK), F32)
        small = jnp.zeros((height, BLOCK), F32)
        for b in range(blocks):
            weights = halves[b * BLOCK : (b + 1) * BLOCK, :]
            total = total + dot(split[b, :, :BLOCK], weights)
            small = small + dot(split[b, :, BLOCK:], weights[:, :BLOCK])
        sums = total[:, :BLOCK] + total[:, BLOCK:] + small
        sum_send[it] = sums.T[0:8]
        sends = [
            pltpu.make_async_remote_copy(
                src_ref=sum_send.at[it], dst_ref=sum_recv.at[it, k],
                send_sem=sum_ss.at[it, k], recv_sem=sum_rs.at[it, k],
                device_id={"cols": peers[k - 1]}, device_id_type=MESH,
            )
            for k in range(1, col_count)
        ]
        for send in sends:
            send.start()

        for b in range(blocks):
            at = slice(b * BLOCK, (b + 1) * BLOCK)
            both = dot(split[b], halves[length : length + 2 * BLOCK, :]) + dot(
                split[b, :, :BLOCK], halves[length + 2 * BLOCK : length + 3 * BLOCK, :]
            )
            on[:, at] = both[:, :BLOCK]
            bk[:, at] = both[:, BLOCK:]

        entering = hop_here[:, 0:1] * sum_send[it]
        for k in range(1, col_count):
            sends[k - 1].wait_recv()
            entering = entering + hop_here[:, k : k + 1] * sum_recv[it, k]
        car[...] = sums + jnp.dot(
            transposed(entering), exact[0:BLOCK, :], precision=EXACT, preferred_element_type=F32
        )

        def solve(t, carry):
            at = rows_of(t)
            inner = rows_of(t + 1)
            enter = car[at, :]
            for b in range(blocks):
                cells = slice(b * BLOCK, (b + 1) * BLOCK)
                r = res[at, cells]
                o = on[at, cells] + rising * enter[:, 8 + b : 9 + b]
                w = bk[at, cells] + falling * enter[:, 40 + b : 41 + b]
                wet = wd[inner, cells] > 0.0
                d = jnp.where(wet, gain * (o + w - r), 0.0)
                if last:
                    lev[at, cells] = math.sqrt(REACH) * (lev[at, cells] + d)
                    continue
                if it == 0:
                    lev[at, cells] = d
                else:
                    lev[at, cells] = lev[at, cells] + d
                dl[inner, cells] = d
                flux_e = (w - r) * (1.0 / decay) - o
                flux_w = w - (o - r) * (1.0 / decay)
                scale = stiffness * gain * lag
                res[at, cells] = (
                    r - d + scale * (ce[at, cells] * flux_e - cw[at, cells] * flux_w)
                )
            return carry

        if last:
            lax.fori_loop(0, tiles, solve, 0)
            for send in sends:
                send.wait_send()
            break

        solve(0, 0)
        solve(tiles - 1, 0)
        drow_send[it, 0] = dl[PAD : PAD + 1, :]
        drow_send[it, 1] = dl[PAD + height - 1 : PAD + height, :]
        d_halo = copies(
            drow_send.at[it], drow_recv.at[it], d_ss.at[it], d_rs.at[it], "rows", row
        )
        start(d_halo, has_n, has_s)
        lax.fori_loop(1, tiles - 1, solve, 0)

        def cross(t, carry):
            at = rows_of(t)
            here, north, south = three(dl, t)
            value = res[at, :] - cn[at, :] * (here - north) - cs[at, :] * (here - south)
            res[at, :] = jnp.where(wd[rows_of(t + 1), :] > 0.0, value, 0.0)
            return carry

        lax.fori_loop(1, tiles - 1, cross, 0)
        finish(d_halo, drow_recv.at[it], has_n, has_s)
        dl[PAD - 1 : PAD, :] = drow_recv[it, 0]
        dl[PAD + height : PAD + height + 1, :] = drow_recv[it, 1]
        cross(0, 0)
        cross(tiles - 1, 0)
        for send in sends:
            send.wait_send()

    out = pltpu.make_async_copy(lev, out_hbm, out_sem.at[1])
    out.start()
    out.wait()
    pred_out.wait()


def hand_on(pred_in, level_in, pred_out, level_out, sem):
    moves = [pltpu.make_async_copy(pred_in.at[k], pred_out.at[k], sem.at[k]) for k in range(4)]
    moves.append(pltpu.make_async_copy(level_in, level_out, sem.at[4]))
    for move in moves:
        move.start()
    for move in moves:
        move.wait()


def per_device(row_count, col_count, velocity, layer_gap, surface, basin_depth, ocean_mask):
    height, length = surface.shape
    halves, exact = tables(length, col_count)
    padded = pltpu.VMEM((height + 2 * PAD, length), F32)
    plain = pltpu.VMEM((height, length), F32)
    tile = pltpu.VMEM((height, BLOCK), F32)
    dma = pltpu.SemaphoreType.DMA
    anywhere = pl.BlockSpec(memory_space=pl.ANY)
    predicted, level = pl.pallas_call(
        functools.partial(kernel, row_count, col_count, height, length),
        out_shape=(
            jax.ShapeDtypeStruct(velocity.shape, F32),
            jax.ShapeDtypeStruct(surface.shape, F32),
        ),
        in_specs=[anywhere] * 7,
        out_specs=(anywhere, anywhere),
        scratch_shapes=[
            pltpu.VMEM((4, height + 2 * PAD, length), F32),
            padded, padded, pltpu.VMEM((height, length), jnp.int32), plain,
            pltpu.VMEM(halves.shape, F32), pltpu.VMEM(halves.shape, jnp.bfloat16), pltpu.VMEM(exact.shape, F32),
            pltpu.VMEM((2, 4, height, BLOCK), F32), pltpu.VMEM((2, height, BLOCK), F32),
            pltpu.VMEM((2, height, BLOCK), F32), pltpu.VMEM((2, height, BLOCK), jnp.int32),
            pltpu.VMEM((length // BLOCK, height, 2 * BLOCK), jnp.bfloat16),
            pltpu.VMEM((4, height, length), F32),
            plain, padded, plain, plain, plain, plain, plain, plain, plain, padded, plain, tile,
            pltpu.VMEM((2, 8, length), F32), pltpu.VMEM((2, 8, length), F32),
            pltpu.VMEM((2, 8, BLOCK), F32), pltpu.VMEM((2, 8, BLOCK), F32),
            tile, tile,
            pltpu.VMEM((2, 1, length), F32), pltpu.VMEM((2, 1, length), F32),
            pltpu.VMEM((2, 8, BLOCK), F32), pltpu.VMEM((2, 8, BLOCK), F32),
            pltpu.VMEM((ITERS, 8, BLOCK), F32), pltpu.VMEM((ITERS, col_count, 8, BLOCK), F32),
            pltpu.VMEM((ITERS, 2, 1, length), F32), pltpu.VMEM((ITERS, 2, 1, length), F32),
            dma((23,)), dma((2,)), dma((2, 2)), dma((2, 2)), dma((2, 2)), dma((2, 2)),
            dma((ITERS, col_count)), dma((ITERS, col_count)), dma((ITERS, 2)), dma((ITERS, 2)),
        ],
        compiler_params=pltpu.CompilerParams(
            collective_id=0, has_side_effects=True, vmem_limit_bytes=60 * 2**20
        ),
    )(velocity, layer_gap, surface, basin_depth, ocean_mask, halves, exact)
    return pl.pallas_call(
        hand_on,
        out_shape=(
            jax.ShapeDtypeStruct(velocity.shape, F32),
            jax.ShapeDtypeStruct(surface.shape, F32),
        ),
        in_specs=[anywhere] * 2,
        out_specs=(anywhere, anywhere),
        scratch_shapes=[dma((5,))],
        compiler_params=pltpu.CompilerParams(vmem_limit_bytes=60 * 2**20),
    )(predicted, level)


def solution(mesh):
    placed = (P(None, "rows", "cols"),) + (P("rows", "cols"),) * 4
    return jax.shard_map(
        functools.partial(per_device, mesh.shape["rows"], mesh.shape["cols"]),
        mesh=mesh,
        in_specs=placed,
        out_specs=(P(None, "rows", "cols"), P("rows", "cols")),
        check_vma=False,
    )
```

```python
import functools
import math

import jax
import jax.numpy as jnp
import numpy as np
from jax import lax
from jax.experimental import pallas as pl
from jax.experimental.pallas import tpu as pltpu
from jax.sharding import PartitionSpec as P

ITERS = 3
REACH = 4096
BLOCK = 128
PAD = 8

coriolis_dt = 0.1
viscous_dt = 0.05
buoyant_dt = 0.2
top_share = 0.3
transport_dt = 0.5
cross_weight = 0.5
F32 = jnp.float32
MESH = pl.DeviceIdType.MESH
EXACT = lax.Precision.HIGHEST


def line_constants():
    base = 1.0 + 2.0 * cross_weight
    stiffness = base * REACH**2
    root = math.sqrt(base * base + 4.0 * base * stiffness)
    lag = (base + root) / (base + 2.0 * stiffness + root)
    gain = 1.0 / (base + 2.0 * stiffness * lag)
    return stiffness, lag, gain


def tables(length, count):
    _, lag, _ = line_constants()
    log = math.log1p(-lag)
    power = lambda n: np.exp(np.asarray(n, np.float64) * log)
    lane = np.arange(BLOCK)
    gap = lane[None, :] - lane[:, None]
    onward = np.where(gap >= 0, power(np.maximum(gap, 0)), 0.0)
    within = np.concatenate([onward, onward.T], axis=1)
    cell = np.arange(length)
    blocks = length // BLOCK
    gather = np.zeros((length, BLOCK))
    gather[:, 0] = gather[:, 3] = power(length - 1 - cell)
    gather[:, 1] = gather[:, 2] = power(cell)
    spread = np.zeros((BLOCK, BLOCK))
    for b in range(blocks):
        west, east = b * BLOCK, (b + 1) * BLOCK
        gather[:west, 8 + b] = power(west - 1 - cell[:west])
        gather[east:, 40 + b] = power(cell[east:] - east)
        spread[0, 8 + b] = spread[2, 8 + b] = power(west)
        spread[1, 40 + b] = spread[3, 40 + b] = power(length - east)
    q = float(power(length * count))
    hop = np.zeros((count, 8, BLOCK))
    for me in range(count):
        for k in range(count):
            p = (me - k) % count
            first, last = float(power(p * length)), float(power((count - 1 - p) * length))
            west_in, east_in = float(power(me * length)), float(power((count - 1 - me) * length))
            hop[me, 0, k] = west_in * q * last / (1 - q * q)
            hop[me, 2, k] = west_in * first / (1 - q * q)
            hop[me, 1, k] = east_in * q * first / (1 - q * q)
            hop[me, 3, k] = east_in * last / (1 - q * q)
            if p < me:
                hop[me, 0, k] += float(power((me - 1 - p) * length))
            if p > me:
                hop[me, 1, k] += float(power((p - me - 1) * length))
    edge = np.zeros((8, BLOCK))
    edge[0] = power(lane + 1)
    edge[1] = power(BLOCK - lane)
    def split(a):
        high = np.asarray(a, np.float32).astype(jnp.bfloat16)
        return high, (a - high.astype(np.float64)).astype(np.float32).astype(jnp.bfloat16)

    within_high, within_low = split(within)
    halves = np.concatenate(
        [np.concatenate(split(gather), axis=1), within_high, within_high, within_low],
        axis=0,
    )
    exact = np.concatenate([spread, edge, hop.reshape(count * 8, BLOCK)]).astype(np.float32)
    return halves.astype(np.float32), exact


def transposed(rows8):
    return jnp.concatenate([rows8, jnp.zeros((BLOCK - 8, BLOCK), F32)], axis=0).T


def kernel(
    row_count, col_count, height, length,
    vel_hbm, gap_hbm, surf_hbm, depth_hbm, mask_hbm, halves_hbm, exact_hbm,
    pred_hbm, out_hbm,
    vel, gap, wd, mask, surf, wide_halves, halves, exact, vel_col, gap_col, depth_col, mask_col, split, pred, fe, fn, ce, cw, cn, cs, res, on, bk, dl, lev, car,
    row_send, row_recv, col_send, col_recv, colw, cole, frow_send, frow_recv, fcol_send, fcol_recv,
    sum_send, sum_recv, drow_send, drow_recv,
    load_sem, out_sem, halo_ss, halo_rs, fh_ss, fh_rs, sum_ss, sum_rs, d_ss, d_rs,
):
    row = lax.axis_index("rows")
    col = lax.axis_index("cols")
    tiles = height // 8
    blocks = length // BLOCK
    stiffness, lag, gain = line_constants()
    decay = 1.0 - lag

    middle = height - 16
    sources = (
        (depth_hbm, wd, depth_col, PAD, ()),
        (mask_hbm, mask, mask_col, 0, ()),
        (gap_hbm, gap, gap_col, PAD, ()),
        (vel_hbm, vel, vel_col, PAD, (slice(None),)),
    )
    pairs = []
    for start_row, size in ((0, 8), (height - 8, 8)):
        for hbm, held, _, pad, lead in sources:
            pairs.append((
                hbm.at[lead + (pl.ds(start_row, size),)],
                held.at[lead + (pl.ds(pad + start_row, size),)],
            ))
    for side, first in enumerate((0, length - BLOCK)):
        for hbm, _, held, pad, lead in sources:
            pairs.append((
                hbm.at[lead + (slice(None), pl.ds(first, BLOCK))], held.at[side]
            ))
    for hbm, held, _, pad, lead in sources:
        pairs.append((
            hbm.at[lead + (pl.ds(8, middle),)], held.at[lead + (pl.ds(pad + 8, middle),)]
        ))
    pairs += [(surf_hbm, surf), (halves_hbm, wide_halves), (exact_hbm, exact)]
    loads = [
        pltpu.make_async_copy(src, dst, load_sem.at[i]) for i, (src, dst) in enumerate(pairs)
    ]
    for load in loads:
        load.start()

    has_n, has_s = row > 0, row < row_count - 1
    has_w, has_e = col > 0, col < col_count - 1
    peers = [lax.rem(col + k, col_count) for k in range(1, col_count)]
    barrier = pltpu.get_barrier_semaphore()
    for peer in peers:
        pl.semaphore_signal(barrier, inc=1, device_id={"cols": peer}, device_id_type=MESH)

    @pl.when(has_n)
    def _():
        pl.semaphore_signal(barrier, inc=1, device_id={"rows": row - 1}, device_id_type=MESH)

    @pl.when(has_s)
    def _():
        pl.semaphore_signal(barrier, inc=1, device_id={"rows": row + 1}, device_id_type=MESH)

    neighbours = jnp.minimum(row, 1) + jnp.minimum(row_count - 1 - row, 1)
    pl.semaphore_wait(barrier, col_count - 1 + neighbours)

    def copies(send, recv, send_sem, recv_sem, axis, place):
        return [
            pltpu.make_async_remote_copy(
                src_ref=send.at[side], dst_ref=recv.at[1 - side],
                send_sem=send_sem.at[side], recv_sem=recv_sem.at[1 - side],
                device_id={axis: place + (2 * side - 1)}, device_id_type=MESH,
            )
            for side in range(2)
        ]

    def start(pair, low, high):
        pl.when(low)(pair[0].start)
        pl.when(high)(pair[1].start)

    def finish(pair, recv, low, high):
        for side, there in ((0, low), (1, high)):
            @pl.when(there)
            def _():
                pair[1 - side].wait_recv()
                pair[side].wait_send()

            @pl.when(jnp.logical_not(there))
            def _():
                recv[side] = jnp.zeros(recv.shape[1:], F32)

    row_halo = copies(row_send, row_recv, halo_ss.at[0], halo_rs.at[0], "rows", row)
    col_halo = copies(col_send, col_recv, halo_ss.at[1], halo_rs.at[1], "cols", col)
    frow_halo = copies(frow_send, frow_recv, fh_ss.at[0], fh_rs.at[0], "rows", row)
    fcol_halo = copies(fcol_send, fcol_recv, fh_ss.at[1], fh_rs.at[1], "cols", col)

    for load in loads[:8]:
        load.wait()
    for side, at in ((0, 0), (1, height - 1)):
        for k in range(4):
            row_send[side, k : k + 1, :] = vel[k, PAD + at : PAD + at + 1, :]
        row_send[side, 4:5, :] = gap[PAD + at : PAD + at + 1, :]
        row_send[side, 5:6, :] = (
            wd[PAD + at : PAD + at + 1, :] * mask[at : at + 1, :].astype(F32)
        )
    start(row_halo, has_n, has_s)
    for load in loads[8:16]:
        load.wait()
    lane = lax.broadcasted_iota(jnp.int32, (height, BLOCK), 1)
    for side in range(2):
        columns = [vel_col[side, k] for k in range(4)]
        columns += [gap_col[side], depth_col[side] * mask_col[side].astype(F32)]
        pack = jnp.zeros((height, BLOCK), F32)
        for k, column in enumerate(columns):
            pack = jnp.where(
                lane == k, column if k + side == 0 else pltpu.roll(column, k + side, 1), pack
            )
        col_send[side] = pack.T[0:8]
    start(col_halo, has_w, has_e)
    for load in loads[16:20]:
        load.wait()

    def wetten(t, carry):
        at = pl.ds(pl.multiple_of(PAD + 8 * t, 8), 8)
        wd[at, :] = wd[at, :] * mask[pl.ds(pl.multiple_of(8 * t, 8), 8), :].astype(F32)
        return carry

    lax.fori_loop(0, tiles, wetten, 0)
    fields = [vel.at[0], vel.at[1], vel.at[2], vel.at[3], gap, wd]
    finish(col_halo, col_recv, has_w, has_e)
    colw[...] = transposed(col_recv[0])
    cole[...] = transposed(col_recv[1])

    wide = lax.broadcasted_iota(jnp.int32, (8, length), 1)
    at_west, at_east = wide == 0, wide == length - 1

    def west_of(x, edge_column):
        return jnp.where(at_west, edge_column, pltpu.roll(x, 1, 1))

    def east_of(x, edge_column):
        return jnp.where(at_east, edge_column, pltpu.roll(x, length - 1, 1))

    def rows_of(t):
        return pl.ds(pl.multiple_of(8 * t, 8), 8)

    sub = lax.broadcasted_iota(jnp.int32, (8, length), 0)

    def three(ref, t):
        before = ref[rows_of(t), :]
        here = ref[rows_of(t + 1), :]
        after = ref[rows_of(t + 2), :]
        north = pltpu.roll(jnp.where(sub == 7, before, here), 1, 0)
        south = pltpu.roll(jnp.where(sub == 0, after, here), 7, 0)
        return here, north, south

    def momentum(t, carry):
        at = rows_of(t)
        depth_here = wd[rows_of(t + 1), :]
        wet = jnp.where(depth_here > 0.0, 1.0, 0.0)
        west_halo, east_halo = colw[at, :], cole[at, :]
        gap_here, gap_north, gap_south = three(gap, t)
        slope_east = 0.5 * (
            east_of(gap_here, east_halo[:, 4:5]) - west_of(gap_here, west_halo[:, 4:5])
        )
        slope_north = 0.5 * (gap_south - gap_north)
        for pair in range(2):
            parts = []
            for side in range(2):
                k = 2 * pair + side
                here, north, south = three(vel.at[k], t)
                lap = (
                    east_of(here, east_halo[:, k : k + 1])
                    + west_of(here, west_halo[:, k : k + 1])
                    + south + north - 4.0 * here
                )
                parts.append(here + viscous_dt * lap)
            u, v = vel[2 * pair, rows_of(t + 1), :], vel[2 * pair + 1, rows_of(t + 1), :]
            east = parts[0] + coriolis_dt * v
            north_part = parts[1] - coriolis_dt * u
            if pair == 1:
                east = east - buoyant_dt * slope_east
                north_part = north_part - buoyant_dt * slope_north
            pred[2 * pair, at, :] = wet * east
            pred[2 * pair + 1, at, :] = wet * north_part
        fe[at, :] = depth_here * (top_share * pred[0, at, :] + (1.0 - top_share) * pred[2, at, :])
        fn[rows_of(t + 1), :] = depth_here * (
            top_share * pred[1, at, :] + (1.0 - top_share) * pred[3, at, :]
        )
        return carry

    lax.fori_loop(1, tiles - 1, momentum, 0)
    finish(row_halo, row_recv, has_n, has_s)
    for k, field in enumerate(fields):
        field[PAD - 1 : PAD, :] = row_recv[0, k : k + 1, :]
        field[PAD + height : PAD + height + 1, :] = row_recv[1, k : k + 1, :]
    outer = lambda i, carry: momentum(i * (tiles - 1), carry)
    lax.fori_loop(0, 2, outer, 0)
    pred_out = pltpu.make_async_copy(pred, pred_hbm, out_sem.at[0])
    pred_out.start()

    frow_send[0] = fn[PAD : PAD + 1, :]
    frow_send[1] = fn[PAD + height - 1 : PAD + height, :]
    start(frow_halo, has_n, has_s)
    fcol_send[0] = fe[:, 0:BLOCK].T[0:8]
    fcol_send[1] = pltpu.roll(fe[:, length - BLOCK : length], 1, 1).T[0:8]
    start(fcol_halo, has_w, has_e)

    def conductances(t, carry):
        at = rows_of(t)
        here, north, south = three(wd, t)
        ce[at, :] = jnp.sqrt(here * east_of(here, cole[at, 5:6]))
        cw[at, :] = jnp.sqrt(here * west_of(here, colw[at, 5:6]))
        cn[at, :] = cross_weight * jnp.sqrt(here * north)
        cs[at, :] = cross_weight * jnp.sqrt(here * south)
        return carry

    lax.fori_loop(0, tiles, conductances, 0)
    for load in loads[20:]:
        load.wait()

    def narrow(t, carry):
        at = pl.ds(pl.multiple_of(BLOCK * t, BLOCK), BLOCK)
        halves[at, :] = wide_halves[at, :].astype(jnp.bfloat16)
        return carry

    lax.fori_loop(0, blocks + 3, narrow, 0)
    finish(frow_halo, frow_recv, has_n, has_s)
    finish(fcol_halo, fcol_recv, has_w, has_e)
    fn[PAD - 1 : PAD, :] = frow_recv[0]
    fn[PAD + height : PAD + height + 1, :] = frow_recv[1]
    colw[...] = transposed(fcol_recv[0])
    cole[...] = transposed(fcol_recv[1])

    def force(t, carry):
        at = rows_of(t)
        east_flux = fe[at, :]
        _, north, south = three(fn, t)
        divergence = 0.5 * (
            east_of(east_flux, cole[at, 0:1]) - west_of(east_flux, colw[at, 0:1])
        ) + 0.5 * (south - north)
        wet = wd[rows_of(t + 1), :] > 0.0
        res[at, :] = jnp.where(wet, surf[at, :] - transport_dt * divergence, 0.0)
        return carry

    lax.fori_loop(0, tiles, force, 0)

    hop_here = exact[pl.ds(pl.multiple_of(BLOCK + 8 + 8 * col, 8), 8), :]
    rising = jnp.broadcast_to(exact[BLOCK : BLOCK + 1, :], (8, BLOCK))
    falling = jnp.broadcast_to(exact[BLOCK + 1 : BLOCK + 2, :], (8, BLOCK))
    dot = functools.partial(jnp.dot, preferred_element_type=F32)
    for it in range(ITERS):
        last = it + 1 == ITERS
        for b in range(blocks):
            at = slice(b * BLOCK, (b + 1) * BLOCK)
            high = res[:, at].astype(jnp.bfloat16)
            split[b, :, :BLOCK] = high
            split[b, :, BLOCK:] = (res[:, at] - high.astype(F32)).astype(jnp.bfloat16)
        total = jnp.zeros((height, 2 * BLOCK), F32)
        small = jnp.zeros((height, BLOCK), F32)
        for b in range(blocks):
            weights = halves[b * BLOCK : (b + 1) * BLOCK, :]
            total = total + dot(split[b, :, :BLOCK], weights)
            small = small + dot(split[b, :, BLOCK:], weights[:, :BLOCK])
        sums = total[:, :BLOCK] + total[:, BLOCK:] + small
        sum_send[it] = sums.T[0:8]
        sends = [
            pltpu.make_async_remote_copy(
                src_ref=sum_send.at[it], dst_ref=sum_recv.at[it, k],
                send_sem=sum_ss.at[it, k], recv_sem=sum_rs.at[it, k],
                device_id={"cols": peers[k - 1]}, device_id_type=MESH,
            )
            for k in range(1, col_count)
        ]
        for send in sends:
            send.start()

        for b in range(blocks):
            at = slice(b * BLOCK, (b + 1) * BLOCK)
            both = dot(split[b], halves[length : length + 2 * BLOCK, :]) + dot(
                split[b, :, :BLOCK], halves[length + 2 * BLOCK : length + 3 * BLOCK, :]
            )
            on[:, at] = both[:, :BLOCK]
            bk[:, at] = both[:, BLOCK:]

        entering = hop_here[:, 0:1] * sum_send[it]
        for k in range(1, col_count):
            sends[k - 1].wait_recv()
            entering = entering + hop_here[:, k : k + 1] * sum_recv[it, k]
        car[...] = sums + jnp.dot(
            transposed(entering), exact[0:BLOCK, :], precision=EXACT, preferred_element_type=F32
        )

        def solve(t, carry):
            at = rows_of(t)
            inner = rows_of(t + 1)
            enter = car[at, :]
            for b in range(blocks):
                cells = slice(b * BLOCK, (b + 1) * BLOCK)
                r = res[at, cells]
                o = on[at, cells] + rising * enter[:, 8 + b : 9 + b]
                w = bk[at, cells] + falling * enter[:, 40 + b : 41 + b]
                wet = wd[inner, cells] > 0.0
                d = jnp.where(wet, gain * (o + w - r), 0.0)
                if last:
                    lev[at, cells] = math.sqrt(REACH) * (lev[at, cells] + d)
                    continue
                if it == 0:
                    lev[at, cells] = d
                else:
                    lev[at, cells] = lev[at, cells] + d
                dl[inner, cells] = d
                flux_e = (w - r) * (1.0 / decay) - o
                flux_w = w - (o - r) * (1.0 / decay)
                scale = stiffness * gain * lag
                res[at, cells] = (
                    r - d + scale * (ce[at, cells] * flux_e - cw[at, cells] * flux_w)
                )
            return carry

        if last:
            lax.fori_loop(0, tiles, solve, 0)
            for send in sends:
                send.wait_send()
            break

        solve(0, 0)
        solve(tiles - 1, 0)
        drow_send[it, 0] = dl[PAD : PAD + 1, :]
        drow_send[it, 1] = dl[PAD + height - 1 : PAD + height, :]
        d_halo = copies(
            drow_send.at[it], drow_recv.at[it], d_ss.at[it], d_rs.at[it], "rows", row
        )
        start(d_halo, has_n, has_s)
        lax.fori_loop(1, tiles - 1, solve, 0)

        def cross(t, carry):
            at = rows_of(t)
            here, north, south = three(dl, t)
            value = res[at, :] - cn[at, :] * (here - north) - cs[at, :] * (here - south)
            res[at, :] = jnp.where(wd[rows_of(t + 1), :] > 0.0, value, 0.0)
            return carry

        lax.fori_loop(1, tiles - 1, cross, 0)
        finish(d_halo, drow_recv.at[it], has_n, has_s)
        dl[PAD - 1 : PAD, :] = drow_recv[it, 0]
        dl[PAD + height : PAD + height + 1, :] = drow_recv[it, 1]
        cross(0, 0)
        cross(tiles - 1, 0)
        for send in sends:
            send.wait_send()

    out = pltpu.make_async_copy(lev, out_hbm, out_sem.at[1])
    out.start()
    out.wait()
    pred_out.wait()


def hand_on(pred_in, level_in, pred_out, level_out, held, in_sem, out_sem):
    sources = [pred_in.at[k] for k in range(4)] + [level_in]
    targets = [pred_out.at[k] for k in range(4)] + [level_out]
    reads = [
        pltpu.make_async_copy(src, held.at[k], in_sem.at[k]) for k, src in enumerate(sources)
    ]
    writes = [
        pltpu.make_async_copy(held.at[k], dst, out_sem.at[k]) for k, dst in enumerate(targets)
    ]
    for read in reads:
        read.start()
    for read, write in zip(reads, writes):
        read.wait()
        write.start()
    for write in writes:
        write.wait()


def per_device(row_count, col_count, velocity, layer_gap, surface, basin_depth, ocean_mask):
    height, length = surface.shape
    halves, exact = tables(length, col_count)
    padded = pltpu.VMEM((height + 2 * PAD, length), F32)
    plain = pltpu.VMEM((height, length), F32)
    tile = pltpu.VMEM((height, BLOCK), F32)
    dma = pltpu.SemaphoreType.DMA
    anywhere = pl.BlockSpec(memory_space=pl.ANY)
    predicted, level = pl.pallas_call(
        functools.partial(kernel, row_count, col_count, height, length),
        out_shape=(
            jax.ShapeDtypeStruct(velocity.shape, F32),
            jax.ShapeDtypeStruct(surface.shape, F32),
        ),
        in_specs=[anywhere] * 7,
        out_specs=(anywhere, anywhere),
        scratch_shapes=[
            pltpu.VMEM((4, height + 2 * PAD, length), F32),
            padded, padded, pltpu.VMEM((height, length), jnp.int32), plain,
            pltpu.VMEM(halves.shape, F32), pltpu.VMEM(halves.shape, jnp.bfloat16), pltpu.VMEM(exact.shape, F32),
            pltpu.VMEM((2, 4, height, BLOCK), F32), pltpu.VMEM((2, height, BLOCK), F32),
            pltpu.VMEM((2, height, BLOCK), F32), pltpu.VMEM((2, height, BLOCK), jnp.int32),
            pltpu.VMEM((length // BLOCK, height, 2 * BLOCK), jnp.bfloat16),
            pltpu.VMEM((4, height, length), F32),
            plain, padded, plain, plain, plain, plain, plain, plain, plain, padded, plain, tile,
            pltpu.VMEM((2, 8, length), F32), pltpu.VMEM((2, 8, length), F32),
            pltpu.VMEM((2, 8, BLOCK), F32), pltpu.VMEM((2, 8, BLOCK), F32),
            tile, tile,
            pltpu.VMEM((2, 1, length), F32), pltpu.VMEM((2, 1, length), F32),
            pltpu.VMEM((2, 8, BLOCK), F32), pltpu.VMEM((2, 8, BLOCK), F32),
            pltpu.VMEM((ITERS, 8, BLOCK), F32), pltpu.VMEM((ITERS, col_count, 8, BLOCK), F32),
            pltpu.VMEM((ITERS, 2, 1, length), F32), pltpu.VMEM((ITERS, 2, 1, length), F32),
            dma((23,)), dma((2,)), dma((2, 2)), dma((2, 2)), dma((2, 2)), dma((2, 2)),
            dma((ITERS, col_count)), dma((ITERS, col_count)), dma((ITERS, 2)), dma((ITERS, 2)),
        ],
        compiler_params=pltpu.CompilerParams(
            collective_id=0, has_side_effects=True, vmem_limit_bytes=60 * 2**20
        ),
    )(velocity, layer_gap, surface, basin_depth, ocean_mask, halves, exact)
    return pl.pallas_call(
        hand_on,
        out_shape=(
            jax.ShapeDtypeStruct(velocity.shape, F32),
            jax.ShapeDtypeStruct(surface.shape, F32),
        ),
        in_specs=[anywhere] * 2,
        out_specs=(anywhere, anywhere),
        scratch_shapes=[pltpu.VMEM((5, height, length), F32), dma((5,)), dma((5,))],
        compiler_params=pltpu.CompilerParams(vmem_limit_bytes=60 * 2**20),
    )(predicted, level)


def solution(mesh):
    placed = (P(None, "rows", "cols"),) + (P("rows", "cols"),) * 4
    return jax.shard_map(
        functools.partial(per_device, mesh.shape["rows"], mesh.shape["cols"]),
        mesh=mesh,
        in_specs=placed,
        out_specs=(P(None, "rows", "cols"), P("rows", "cols")),
        check_vma=False,
    )
```

```python
import functools
import math

import jax
import jax.numpy as jnp
import numpy as np
from jax import lax
from jax.experimental import pallas as pl
from jax.experimental.pallas import tpu as pltpu
from jax.sharding import PartitionSpec as P

ITERS = 3
REACH = 4096
BLOCK = 128
PAD = 8

coriolis_dt = 0.1
viscous_dt = 0.05
buoyant_dt = 0.2
top_share = 0.3
transport_dt = 0.5
cross_weight = 0.5
F32 = jnp.float32
MESH = pl.DeviceIdType.MESH
EXACT = lax.Precision.HIGHEST


def line_constants():
    base = 1.0 + 2.0 * cross_weight
    stiffness = base * REACH**2
    root = math.sqrt(base * base + 4.0 * base * stiffness)
    lag = (base + root) / (base + 2.0 * stiffness + root)
    gain = 1.0 / (base + 2.0 * stiffness * lag)
    return stiffness, lag, gain


def tables(length, count):
    _, lag, _ = line_constants()
    log = math.log1p(-lag)
    power = lambda n: np.exp(np.asarray(n, np.float64) * log)
    lane = np.arange(BLOCK)
    gap = lane[None, :] - lane[:, None]
    onward = np.where(gap >= 0, power(np.maximum(gap, 0)), 0.0)
    within = np.concatenate([onward, onward.T], axis=1)
    cell = np.arange(length)
    blocks = length // BLOCK
    gather = np.zeros((length, BLOCK))
    gather[:, 0] = gather[:, 3] = power(length - 1 - cell)
    gather[:, 1] = gather[:, 2] = power(cell)
    spread = np.zeros((BLOCK, BLOCK))
    for b in range(blocks):
        west, east = b * BLOCK, (b + 1) * BLOCK
        gather[:west, 8 + b] = power(west - 1 - cell[:west])
        gather[east:, 40 + b] = power(cell[east:] - east)
        spread[0, 8 + b] = spread[2, 8 + b] = power(west)
        spread[1, 40 + b] = spread[3, 40 + b] = power(length - east)
    q = float(power(length * count))
    hop = np.zeros((count, 8, BLOCK))
    for me in range(count):
        for k in range(count):
            p = (me - k) % count
            first, last = float(power(p * length)), float(power((count - 1 - p) * length))
            west_in, east_in = float(power(me * length)), float(power((count - 1 - me) * length))
            hop[me, 0, k] = west_in * q * last / (1 - q * q)
            hop[me, 2, k] = west_in * first / (1 - q * q)
            hop[me, 1, k] = east_in * q * first / (1 - q * q)
            hop[me, 3, k] = east_in * last / (1 - q * q)
            if p < me:
                hop[me, 0, k] += float(power((me - 1 - p) * length))
            if p > me:
                hop[me, 1, k] += float(power((p - me - 1) * length))
    edge = np.zeros((8, BLOCK))
    edge[0] = power(lane + 1)
    edge[1] = power(BLOCK - lane)
    def split(a):
        high = np.asarray(a, np.float32).astype(jnp.bfloat16)
        return high, (a - high.astype(np.float64)).astype(np.float32).astype(jnp.bfloat16)

    within_high, within_low = split(within)
    halves = np.concatenate(
        [np.concatenate(split(gather), axis=1), within_high, within_high, within_low],
        axis=0,
    )
    exact = np.concatenate([spread, edge, hop.reshape(count * 8, BLOCK)]).astype(np.float32)
    return halves.astype(np.float32), exact


def transposed(rows8):
    return jnp.concatenate([rows8, jnp.zeros((BLOCK - 8, BLOCK), F32)], axis=0).T


def kernel(
    row_count, col_count, height, length,
    vel_hbm, gap_hbm, surf_hbm, depth_hbm, mask_hbm, halves_hbm, exact_hbm,
    pred_hbm, out_hbm,
    vel, gap, wd, mask, surf, wide_halves, halves, exact, vel_col, gap_col, depth_col, mask_col, split, pred, fe, fn, ce, cw, cn, cs, res, on, bk, dl, lev, car,
    row_send, row_recv, col_send, col_recv, colw, cole, frow_send, frow_recv, fcol_send, fcol_recv,
    sum_send, sum_recv, drow_send, drow_recv,
    load_sem, out_sem, halo_ss, halo_rs, fh_ss, fh_rs, sum_ss, sum_rs, d_ss, d_rs,
):
    row = lax.axis_index("rows")
    col = lax.axis_index("cols")
    tiles = height // 8
    blocks = length // BLOCK
    stiffness, lag, gain = line_constants()
    decay = 1.0 - lag

    middle = height - 16
    sources = (
        (depth_hbm, wd, depth_col, PAD, ()),
        (mask_hbm, mask, mask_col, 0, ()),
        (gap_hbm, gap, gap_col, PAD, ()),
        (vel_hbm, vel, vel_col, PAD, (slice(None),)),
    )
    pairs = []
    for start_row, size in ((0, 8), (height - 8, 8)):
        for hbm, held, _, pad, lead in sources:
            pairs.append((
                hbm.at[lead + (pl.ds(start_row, size),)],
                held.at[lead + (pl.ds(pad + start_row, size),)],
            ))
    for side, first in enumerate((0, length - BLOCK)):
        for hbm, _, held, pad, lead in sources:
            pairs.append((
                hbm.at[lead + (slice(None), pl.ds(first, BLOCK))], held.at[side]
            ))
    for hbm, held, _, pad, lead in sources:
        pairs.append((
            hbm.at[lead + (pl.ds(8, middle),)], held.at[lead + (pl.ds(pad + 8, middle),)]
        ))
    pairs += [(surf_hbm, surf), (halves_hbm, wide_halves), (exact_hbm, exact)]
    loads = [
        pltpu.make_async_copy(src, dst, load_sem.at[i]) for i, (src, dst) in enumerate(pairs)
    ]
    for load in loads:
        load.start()

    has_n, has_s = row > 0, row < row_count - 1
    has_w, has_e = col > 0, col < col_count - 1
    peers = [lax.rem(col + k, col_count) for k in range(1, col_count)]
    barrier = pltpu.get_barrier_semaphore()
    for peer in peers:
        pl.semaphore_signal(barrier, inc=1, device_id={"cols": peer}, device_id_type=MESH)

    @pl.when(has_n)
    def _():
        pl.semaphore_signal(barrier, inc=1, device_id={"rows": row - 1}, device_id_type=MESH)

    @pl.when(has_s)
    def _():
        pl.semaphore_signal(barrier, inc=1, device_id={"rows": row + 1}, device_id_type=MESH)

    neighbours = jnp.minimum(row, 1) + jnp.minimum(row_count - 1 - row, 1)
    pl.semaphore_wait(barrier, col_count - 1 + neighbours)

    def copies(send, recv, send_sem, recv_sem, axis, place):
        return [
            pltpu.make_async_remote_copy(
                src_ref=send.at[side], dst_ref=recv.at[1 - side],
                send_sem=send_sem.at[side], recv_sem=recv_sem.at[1 - side],
                device_id={axis: place + (2 * side - 1)}, device_id_type=MESH,
            )
            for side in range(2)
        ]

    def start(pair, low, high):
        pl.when(low)(pair[0].start)
        pl.when(high)(pair[1].start)

    def finish(pair, recv, low, high):
        for side, there in ((0, low), (1, high)):
            @pl.when(there)
            def _():
                pair[1 - side].wait_recv()
                pair[side].wait_send()

            @pl.when(jnp.logical_not(there))
            def _():
                recv[side] = jnp.zeros(recv.shape[1:], F32)

    row_halo = copies(row_send, row_recv, halo_ss.at[0], halo_rs.at[0], "rows", row)
    col_halo = copies(col_send, col_recv, halo_ss.at[1], halo_rs.at[1], "cols", col)
    frow_halo = copies(frow_send, frow_recv, fh_ss.at[0], fh_rs.at[0], "rows", row)
    fcol_halo = copies(fcol_send, fcol_recv, fh_ss.at[1], fh_rs.at[1], "cols", col)

    for load in loads[:8]:
        load.wait()
    for side, at in ((0, 0), (1, height - 1)):
        for k in range(4):
            row_send[side, k : k + 1, :] = vel[k, PAD + at : PAD + at + 1, :]
        row_send[side, 4:5, :] = gap[PAD + at : PAD + at + 1, :]
        row_send[side, 5:6, :] = (
            wd[PAD + at : PAD + at + 1, :] * mask[at : at + 1, :].astype(F32)
        )
    start(row_halo, has_n, has_s)
    for load in loads[8:16]:
        load.wait()
    lane = lax.broadcasted_iota(jnp.int32, (height, BLOCK), 1)
    for side in range(2):
        columns = [vel_col[side, k] for k in range(4)]
        columns += [gap_col[side], depth_col[side] * mask_col[side].astype(F32)]
        pack = jnp.zeros((height, BLOCK), F32)
        for k, column in enumerate(columns):
            pack = jnp.where(
                lane == k, column if k + side == 0 else pltpu.roll(column, k + side, 1), pack
            )
        col_send[side] = pack.T[0:8]
    start(col_halo, has_w, has_e)
    for load in loads[16:20]:
        load.wait()

    def wetten(t, carry):
        at = pl.ds(pl.multiple_of(PAD + 8 * t, 8), 8)
        wd[at, :] = wd[at, :] * mask[pl.ds(pl.multiple_of(8 * t, 8), 8), :].astype(F32)
        return carry

    lax.fori_loop(0, tiles, wetten, 0)
    fields = [vel.at[0], vel.at[1], vel.at[2], vel.at[3], gap, wd]
    finish(col_halo, col_recv, has_w, has_e)
    colw[...] = transposed(col_recv[0])
    cole[...] = transposed(col_recv[1])

    wide = lax.broadcasted_iota(jnp.int32, (8, length), 1)
    at_west, at_east = wide == 0, wide == length - 1

    def west_of(x, edge_column):
        return jnp.where(at_west, edge_column, pltpu.roll(x, 1, 1))

    def east_of(x, edge_column):
        return jnp.where(at_east, edge_column, pltpu.roll(x, length - 1, 1))

    def rows_of(t):
        return pl.ds(pl.multiple_of(8 * t, 8), 8)

    sub = lax.broadcasted_iota(jnp.int32, (8, length), 0)

    def three(ref, t):
        before = ref[rows_of(t), :]
        here = ref[rows_of(t + 1), :]
        after = ref[rows_of(t + 2), :]
        north = pltpu.roll(jnp.where(sub == 7, before, here), 1, 0)
        south = pltpu.roll(jnp.where(sub == 0, after, here), 7, 0)
        return here, north, south

    def momentum(t, carry):
        at = rows_of(t)
        depth_here = wd[rows_of(t + 1), :]
        wet = jnp.where(depth_here > 0.0, 1.0, 0.0)
        west_halo, east_halo = colw[at, :], cole[at, :]
        gap_here, gap_north, gap_south = three(gap, t)
        slope_east = 0.5 * (
            east_of(gap_here, east_halo[:, 4:5]) - west_of(gap_here, west_halo[:, 4:5])
        )
        slope_north = 0.5 * (gap_south - gap_north)
        for pair in range(2):
            parts = []
            for side in range(2):
                k = 2 * pair + side
                here, north, south = three(vel.at[k], t)
                lap = (
                    east_of(here, east_halo[:, k : k + 1])
                    + west_of(here, west_halo[:, k : k + 1])
                    + south + north - 4.0 * here
                )
                parts.append(here + viscous_dt * lap)
            u, v = vel[2 * pair, rows_of(t + 1), :], vel[2 * pair + 1, rows_of(t + 1), :]
            east = parts[0] + coriolis_dt * v
            north_part = parts[1] - coriolis_dt * u
            if pair == 1:
                east = east - buoyant_dt * slope_east
                north_part = north_part - buoyant_dt * slope_north
            pred[2 * pair, at, :] = wet * east
            pred[2 * pair + 1, at, :] = wet * north_part
        fe[at, :] = depth_here * (top_share * pred[0, at, :] + (1.0 - top_share) * pred[2, at, :])
        fn[rows_of(t + 1), :] = depth_here * (
            top_share * pred[1, at, :] + (1.0 - top_share) * pred[3, at, :]
        )
        return carry

    lax.fori_loop(1, tiles - 1, momentum, 0)
    finish(row_halo, row_recv, has_n, has_s)
    for k, field in enumerate(fields):
        field[PAD - 1 : PAD, :] = row_recv[0, k : k + 1, :]
        field[PAD + height : PAD + height + 1, :] = row_recv[1, k : k + 1, :]
    outer = lambda i, carry: momentum(i * (tiles - 1), carry)
    lax.fori_loop(0, 2, outer, 0)
    pred_out = pltpu.make_async_copy(pred, pred_hbm, out_sem.at[0])
    pred_out.start()

    frow_send[0] = fn[PAD : PAD + 1, :]
    frow_send[1] = fn[PAD + height - 1 : PAD + height, :]
    start(frow_halo, has_n, has_s)
    fcol_send[0] = fe[:, 0:BLOCK].T[0:8]
    fcol_send[1] = pltpu.roll(fe[:, length - BLOCK : length], 1, 1).T[0:8]
    start(fcol_halo, has_w, has_e)

    def conductances(t, carry):
        at = rows_of(t)
        here, north, south = three(wd, t)
        ce[at, :] = jnp.sqrt(here * east_of(here, cole[at, 5:6]))
        cw[at, :] = jnp.sqrt(here * west_of(here, colw[at, 5:6]))
        cn[at, :] = cross_weight * jnp.sqrt(here * north)
        cs[at, :] = cross_weight * jnp.sqrt(here * south)
        return carry

    lax.fori_loop(0, tiles, conductances, 0)
    for load in loads[20:]:
        load.wait()

    def narrow(t, carry):
        at = pl.ds(pl.multiple_of(BLOCK * t, BLOCK), BLOCK)
        halves[at, :] = wide_halves[at, :].astype(jnp.bfloat16)
        return carry

    lax.fori_loop(0, blocks + 3, narrow, 0)
    finish(frow_halo, frow_recv, has_n, has_s)
    finish(fcol_halo, fcol_recv, has_w, has_e)
    fn[PAD - 1 : PAD, :] = frow_recv[0]
    fn[PAD + height : PAD + height + 1, :] = frow_recv[1]
    colw[...] = transposed(fcol_recv[0])
    cole[...] = transposed(fcol_recv[1])

    def force(t, carry):
        at = rows_of(t)
        east_flux = fe[at, :]
        _, north, south = three(fn, t)
        divergence = 0.5 * (
            east_of(east_flux, cole[at, 0:1]) - west_of(east_flux, colw[at, 0:1])
        ) + 0.5 * (south - north)
        wet = wd[rows_of(t + 1), :] > 0.0
        res[at, :] = jnp.where(wet, surf[at, :] - transport_dt * divergence, 0.0)
        return carry

    lax.fori_loop(0, tiles, force, 0)

    hop_here = exact[pl.ds(pl.multiple_of(BLOCK + 8 + 8 * col, 8), 8), :]
    rising = jnp.broadcast_to(exact[BLOCK : BLOCK + 1, :], (8, BLOCK))
    falling = jnp.broadcast_to(exact[BLOCK + 1 : BLOCK + 2, :], (8, BLOCK))
    dot = functools.partial(jnp.dot, preferred_element_type=F32)
    for it in range(ITERS):
        last = it + 1 == ITERS
        for b in range(blocks):
            at = slice(b * BLOCK, (b + 1) * BLOCK)
            high = res[:, at].astype(jnp.bfloat16)
            split[b, :, :BLOCK] = high
            split[b, :, BLOCK:] = (res[:, at] - high.astype(F32)).astype(jnp.bfloat16)
        total = jnp.zeros((height, 2 * BLOCK), F32)
        small = jnp.zeros((height, BLOCK), F32)
        for b in range(blocks):
            weights = halves[b * BLOCK : (b + 1) * BLOCK, :]
            total = total + dot(split[b, :, :BLOCK], weights)
            small = small + dot(split[b, :, BLOCK:], weights[:, :BLOCK])
        sums = total[:, :BLOCK] + total[:, BLOCK:] + small
        sum_send[it] = sums.T[0:8]
        sends = [
            pltpu.make_async_remote_copy(
                src_ref=sum_send.at[it], dst_ref=sum_recv.at[it, k],
                send_sem=sum_ss.at[it, k], recv_sem=sum_rs.at[it, k],
                device_id={"cols": peers[k - 1]}, device_id_type=MESH,
            )
            for k in range(1, col_count)
        ]
        for send in sends:
            send.start()

        for b in range(blocks):
            at = slice(b * BLOCK, (b + 1) * BLOCK)
            both = dot(split[b], halves[length : length + 2 * BLOCK, :]) + dot(
                split[b, :, :BLOCK], halves[length + 2 * BLOCK : length + 3 * BLOCK, :]
            )
            on[:, at] = both[:, :BLOCK]
            bk[:, at] = both[:, BLOCK:]

        entering = hop_here[:, 0:1] * sum_send[it]
        for k in range(1, col_count):
            sends[k - 1].wait_recv()
            entering = entering + hop_here[:, k : k + 1] * sum_recv[it, k]
        car[...] = sums + jnp.dot(
            transposed(entering), exact[0:BLOCK, :], precision=EXACT, preferred_element_type=F32
        )

        def solve(t, carry):
            at = rows_of(t)
            inner = rows_of(t + 1)
            enter = car[at, :]
            for b in range(blocks):
                cells = slice(b * BLOCK, (b + 1) * BLOCK)
                r = res[at, cells]
                o = on[at, cells] + rising * enter[:, 8 + b : 9 + b]
                w = bk[at, cells] + falling * enter[:, 40 + b : 41 + b]
                wet = wd[inner, cells] > 0.0
                d = jnp.where(wet, gain * (o + w - r), 0.0)
                if last:
                    lev[at, cells] = math.sqrt(REACH) * (lev[at, cells] + d)
                    continue
                if it == 0:
                    lev[at, cells] = d
                else:
                    lev[at, cells] = lev[at, cells] + d
                dl[inner, cells] = d
                flux_e = (w - r) * (1.0 / decay) - o
                flux_w = w - (o - r) * (1.0 / decay)
                scale = stiffness * gain * lag
                res[at, cells] = (
                    r - d + scale * (ce[at, cells] * flux_e - cw[at, cells] * flux_w)
                )
            return carry

        if last:
            lax.fori_loop(0, tiles, solve, 0)
            for send in sends:
                send.wait_send()
            break

        solve(0, 0)
        solve(tiles - 1, 0)
        drow_send[it, 0] = dl[PAD : PAD + 1, :]
        drow_send[it, 1] = dl[PAD + height - 1 : PAD + height, :]
        d_halo = copies(
            drow_send.at[it], drow_recv.at[it], d_ss.at[it], d_rs.at[it], "rows", row
        )
        start(d_halo, has_n, has_s)
        lax.fori_loop(1, tiles - 1, solve, 0)

        def cross(t, carry):
            at = rows_of(t)
            here, north, south = three(dl, t)
            value = res[at, :] - cn[at, :] * (here - north) - cs[at, :] * (here - south)
            res[at, :] = jnp.where(wd[rows_of(t + 1), :] > 0.0, value, 0.0)
            return carry

        lax.fori_loop(1, tiles - 1, cross, 0)
        finish(d_halo, drow_recv.at[it], has_n, has_s)
        dl[PAD - 1 : PAD, :] = drow_recv[it, 0]
        dl[PAD + height : PAD + height + 1, :] = drow_recv[it, 1]
        cross(0, 0)
        cross(tiles - 1, 0)
        for send in sends:
            send.wait_send()

    out = pltpu.make_async_copy(lev, out_hbm, out_sem.at[1])
    out.start()
    out.wait()
    pred_out.wait()


def hand_on(pred_in, level_in, pred_out, level_out, held, in_sem, out_sem):
    half = level_in.shape[0] // 2
    bands = [pl.ds(0, half), pl.ds(half, half)]
    sources = [pred_in.at[k, band] for k in range(4) for band in bands]
    sources += [level_in.at[band] for band in bands]
    targets = [pred_out.at[k, band] for k in range(4) for band in bands]
    targets += [level_out.at[band] for band in bands]
    ahead = 3
    reads = [
        pltpu.make_async_copy(src, held.at[k], in_sem.at[k]) for k, src in enumerate(sources)
    ]
    writes = [
        pltpu.make_async_copy(held.at[k], dst, out_sem.at[k]) for k, dst in enumerate(targets)
    ]
    for read in reads[:ahead]:
        read.start()
    for k, (read, write) in enumerate(zip(reads, writes)):
        read.wait()
        write.start()
        if k + ahead < len(reads):
            reads[k + ahead].start()
    for write in writes:
        write.wait()


def per_device(row_count, col_count, velocity, layer_gap, surface, basin_depth, ocean_mask):
    height, length = surface.shape
    halves, exact = tables(length, col_count)
    padded = pltpu.VMEM((height + 2 * PAD, length), F32)
    plain = pltpu.VMEM((height, length), F32)
    tile = pltpu.VMEM((height, BLOCK), F32)
    dma = pltpu.SemaphoreType.DMA
    anywhere = pl.BlockSpec(memory_space=pl.ANY)
    predicted, level = pl.pallas_call(
        functools.partial(kernel, row_count, col_count, height, length),
        out_shape=(
            jax.ShapeDtypeStruct(velocity.shape, F32),
            jax.ShapeDtypeStruct(surface.shape, F32),
        ),
        in_specs=[anywhere] * 7,
        out_specs=(anywhere, anywhere),
        scratch_shapes=[
            pltpu.VMEM((4, height + 2 * PAD, length), F32),
            padded, padded, pltpu.VMEM((height, length), jnp.int32), plain,
            pltpu.VMEM(halves.shape, F32), pltpu.VMEM(halves.shape, jnp.bfloat16), pltpu.VMEM(exact.shape, F32),
            pltpu.VMEM((2, 4, height, BLOCK), F32), pltpu.VMEM((2, height, BLOCK), F32),
            pltpu.VMEM((2, height, BLOCK), F32), pltpu.VMEM((2, height, BLOCK), jnp.int32),
            pltpu.VMEM((length // BLOCK, height, 2 * BLOCK), jnp.bfloat16),
            pltpu.VMEM((4, height, length), F32),
            plain, padded, plain, plain, plain, plain, plain, plain, plain, padded, plain, tile,
            pltpu.VMEM((2, 8, length), F32), pltpu.VMEM((2, 8, length), F32),
            pltpu.VMEM((2, 8, BLOCK), F32), pltpu.VMEM((2, 8, BLOCK), F32),
            tile, tile,
            pltpu.VMEM((2, 1, length), F32), pltpu.VMEM((2, 1, length), F32),
            pltpu.VMEM((2, 8, BLOCK), F32), pltpu.VMEM((2, 8, BLOCK), F32),
            pltpu.VMEM((ITERS, 8, BLOCK), F32), pltpu.VMEM((ITERS, col_count, 8, BLOCK), F32),
            pltpu.VMEM((ITERS, 2, 1, length), F32), pltpu.VMEM((ITERS, 2, 1, length), F32),
            dma((23,)), dma((2,)), dma((2, 2)), dma((2, 2)), dma((2, 2)), dma((2, 2)),
            dma((ITERS, col_count)), dma((ITERS, col_count)), dma((ITERS, 2)), dma((ITERS, 2)),
        ],
        compiler_params=pltpu.CompilerParams(
            collective_id=0, has_side_effects=True, vmem_limit_bytes=60 * 2**20
        ),
    )(velocity, layer_gap, surface, basin_depth, ocean_mask, halves, exact)
    return pl.pallas_call(
        hand_on,
        out_shape=(
            jax.ShapeDtypeStruct(velocity.shape, F32),
            jax.ShapeDtypeStruct(surface.shape, F32),
        ),
        in_specs=[anywhere] * 2,
        out_specs=(anywhere, anywhere),
        scratch_shapes=[pltpu.VMEM((10, height // 2, length), F32), dma((10,)), dma((10,))],
        compiler_params=pltpu.CompilerParams(vmem_limit_bytes=60 * 2**20),
    )(predicted, level)


def solution(mesh):
    placed = (P(None, "rows", "cols"),) + (P("rows", "cols"),) * 4
    return jax.shard_map(
        functools.partial(per_device, mesh.shape["rows"], mesh.shape["cols"]),
        mesh=mesh,
        in_specs=placed,
        out_specs=(P(None, "rows", "cols"), P("rows", "cols")),
        check_vma=False,
    )
```
